32 devices in a mesh: tok: 8 (over z, x), head: 4 (over y, core).
Axes of the slice: x: 2, y: 2, z: 4, core: 2. Of those that a mesh axis runs over, the one named last changes fastest.
Arguments:
- hidden: bfloat16 [1024, 2048], P('tok'), may hold values from -6 to 6
- norm_gain: float32 [2048], replicated, may hold values from 0.1 to 1.9
- w_router: bfloat16 [2048, 8], replicated, may hold values from -0.125 to 0.125
- w_query: bfloat16 [8, 2048, 2048], P(None, None, 'head'), may hold values from -0.125 to 0.125
- w_key: bfloat16 [2048, 2048], P(None, 'head'), may hold values from -0.125 to 0.125
- w_value: bfloat16 [2048, 2048], P(None, 'head'), may hold values from -0.125 to 0.125
- w_out: bfloat16 [8, 2048, 2048], P(None, 'head'), may hold values from -0.125 to 0.125
- key_pool: bfloat16 [64, 128, 2048], P('tok', None, 'head'), may hold values from -48 to 48
- value_pool: bfloat16 [64, 128, 2048], P('tok', None, 'head'), may hold values from -6 to 6
- page_table: int32 [4, 16], replicated, may hold values from 0 to 63, as said below
- request_group: int32 [8], replicated, may hold values from 0 to 3, as said below
- suffix_len: int32 [8], P('tok'), may hold values from 1 to 128, as said below
- att_experts: int32 [1024, 2], P('tok'), may hold values from 0 to 7, all different within a row
Outputs:
- attended: bfloat16 [1024, 2048], P('tok', 'head')
The draws below stay inside these ranges and needn't reach their ends.
Inputs may be any that keep to these rules, and one draw needn't show every extreme that they name: `page_table`: each of the 64 pool pages appears exactly once in the table. `request_group`: each prefix is shared by exactly 2 requests. `suffix_len`: some request has all 128 slots live.
All inputs are finite; a program needn't handle non-finite values.
Results may differ from the reference program's by a relative error of at most 0.015.
Values may be sent and summed in bfloat16 or wider, within the bound.
A program may use at most 128 MiB of HBM per device.

```python
import jax
import jax.numpy as jnp
from jax import lax

D = 2048
KVH = 16
HD = 128
EXPERTS = 8
TOPK = 2
PAGE = 128
GROUPS = 4
SUF = 128
PPG = 16
REQUESTS = 8
GSIZE = 2
POOL = 64
TOKENS = 1024


def draw_page_table(key, part):
    order = jax.random.permutation(jax.random.fold_in(key, 11), POOL)
    return order.reshape(GROUPS, PPG).astype(jnp.int32)


def draw_request_group(key, part):
    order = jax.random.permutation(jax.random.fold_in(key, 12), REQUESTS)
    return (order // GSIZE).astype(jnp.int32)


def draw_suffix_len(key, part):
    lengths = jax.random.randint(jax.random.fold_in(key, 13), (REQUESTS,), 1, SUF + 1)
    full_one = jax.random.randint(jax.random.fold_in(key, 14), (), 0, REQUESTS)
    return lengths.at[full_one].set(SUF).astype(jnp.int32)


def draw_key_pool(key, part):
    shape = (POOL, PAGE, KVH * HD)
    return jnp.clip(jax.random.normal(jax.random.fold_in(key, 24), shape, jnp.float32), -6.0, 6.0).astype(jnp.bfloat16)


def block_scale(stream_key, extent, cuts, least, largest):
    factor_of, own = 1.0, jax.random.fold_in(stream_key, 6)
    for dim, blocks in cuts:
        heights = jnp.exp(jax.random.uniform(jax.random.fold_in(own, dim), (blocks,), jnp.float32, least / len(cuts), largest / len(cuts)))
        factor_of = factor_of * jnp.repeat(heights, extent[dim] // blocks).reshape([-1 if axis == dim else 1 for axis in range(len(extent))])
    return factor_of


def distinct(rng, rows, number_of, top, lift):
    ranking = jax.random.permutation(jax.random.fold_in(rng, 1), number_of)
    boost = ranking
    for power in range(3):
        boost = boost * boost // number_of
    boost = boost * lift // number_of
    tickets = jax.random.randint(jax.random.fold_in(rng, 2), (rows, number_of), 0, 4096) + boost
    fixed_rows = jax.random.permutation(jax.random.fold_in(rng, 3), rows)[jnp.arange(number_of) % rows]
    tickets = jnp.where(jnp.arange(rows)[:, None] == fixed_rows[None, :], 1 << 14, tickets)
    priority = tickets * number_of + jnp.arange(number_of)
    return lax.top_k(priority.astype(jnp.int32), top)[1].astype(jnp.int32)


def centred(stream_key, shape, scale, reach, shards=(), held_as=jnp.bfloat16):
    gain = block_scale(stream_key, shape, shards, -0.22, 0.18) if shards else 1.0
    drawn = jax.random.normal(stream_key, shape, jnp.float32) * scale * gain
    return jnp.minimum(jnp.maximum(drawn, -reach), reach).astype(held_as)


def setup_inputs(seed: int = 0) -> dict:
    streams_of = jax.random.split(jax.random.key(seed), 14)
    return {
        "hidden": centred(streams_of[0], (TOKENS, D), 1.0, 6.0, ((0, 8),)),
        "norm_gain": jnp.clip(1.0 + 0.18 * jax.random.normal(streams_of[1], (D,), jnp.float32), 0.1, 1.9),
        "w_router": centred(streams_of[2], (D, EXPERTS), D ** -0.5, 0.125),
        "w_query": centred(streams_of[3], (EXPERTS, D, KVH * HD), D ** -0.5, 0.125, ((2, 4),)),
        "w_key": centred(streams_of[4], (D, KVH * HD), D ** -0.5, 0.125, ((1, 4),)),
        "w_value": centred(streams_of[5], (D, KVH * HD), D ** -0.5, 0.125, ((1, 4),)),
        "w_out": centred(streams_of[6], (EXPERTS, KVH * HD, D), (KVH * HD) ** -0.5, 0.125, ((1, 4),)),
        "key_pool": draw_key_pool(jax.random.fold_in(streams_of[13], 71), 0),
        "value_pool": centred(streams_of[8], (POOL, PAGE, KVH * HD), 1.0, 6.0, ((0, 8), (2, 4))),
        "page_table": draw_page_table(jax.random.fold_in(streams_of[13], 71), 0),
        "request_group": draw_request_group(jax.random.fold_in(streams_of[13], 71), 0),
        "suffix_len": draw_suffix_len(jax.random.fold_in(streams_of[13], 71), 0),
        "att_experts": distinct(streams_of[12], TOKENS, EXPERTS, TOPK, 2048),
    }


def rotate(values, positions):
    half = values.shape[-1] // 2
    freq = 10000.0 ** (-jnp.arange(half, dtype=jnp.float32) * 2.0 / values.shape[-1])
    angle = positions.astype(jnp.float32)[:, None] * freq[None, :]
    shape = (values.shape[0],) + (1,) * (values.ndim - 2) + (half,)
    cosine = jnp.cos(angle).reshape(shape)
    sine = jnp.sin(angle).reshape(shape)
    first = values[..., :half]
    second = values[..., half:]
    return jnp.concatenate([first * cosine - second * sine, second * cosine + first * sine], axis=-1)

def partial_attention(query, keys, values, mask):
    scale = 1.0 / keys.shape[-1] ** 0.5
    scores = jnp.einsum('rshd,khd->rshk', query.astype(jnp.float32), keys.astype(jnp.float32)) * scale
    if mask is not None:
        scores = jnp.where(mask[:, None, None, :], scores, -1e+30)
    top = lax.optimization_barrier(jnp.max(scores, axis=-1))
    weights = jnp.exp(scores - top[..., None])
    total = lax.optimization_barrier(jnp.sum(weights, axis=-1))
    rounded = lax.optimization_barrier(weights.astype(jnp.bfloat16))
    out = jnp.einsum('rshk,khd->rshd', rounded.astype(jnp.float32), values.astype(jnp.float32))
    return (top, total, out)

def combine(first, second):
    top = jnp.maximum(first[0], second[0])
    scale_a = jnp.exp(first[0] - top)
    scale_b = jnp.exp(second[0] - top)
    total = first[1] * scale_a + second[1] * scale_b
    out = first[2] * scale_a[..., None] + second[2] * scale_b[..., None]
    return (top, total, out)

def reference(hidden, norm_gain, w_router, w_query, w_key, w_value, w_out, key_pool, value_pool, page_table, request_group, suffix_len, att_experts):
    state = hidden.astype(jnp.float32)
    normed = (state * lax.rsqrt(lax.optimization_barrier(jnp.mean(state * state, axis=-1, keepdims=True)) + 1e-06) * norm_gain).astype(jnp.bfloat16)
    logits = jnp.dot(normed, w_router, preferred_element_type=jnp.float32)
    gates = jax.nn.softmax(jnp.take_along_axis(logits, att_experts, axis=1), axis=-1)
    positions = jnp.arange(TOKENS, dtype=jnp.int32) % SUF + PPG * PAGE
    slots = [jnp.zeros((TOKENS, KVH * HD), jnp.float32) for slot in range(TOPK)]
    for expert in range(EXPERTS):
        product = jnp.dot(normed, w_query[expert], preferred_element_type=jnp.float32)
        for slot in range(TOPK):
            slots[slot] = jnp.where(att_experts[:, slot:slot + 1] == expert, product, slots[slot])
    query = jnp.stack(slots, axis=1).reshape(TOKENS, TOPK, KVH, HD)
    query = rotate(query, positions).astype(jnp.bfloat16)
    keys = rotate(jnp.dot(normed, w_key, preferred_element_type=jnp.float32).reshape(TOKENS, KVH, HD), positions).astype(jnp.bfloat16)
    vals = jnp.dot(normed, w_value, preferred_element_type=jnp.float32).astype(jnp.bfloat16).reshape(TOKENS, KVH, HD)

    def one_request(index):
        start = index * SUF
        q_rows = lax.dynamic_slice_in_dim(query, start, SUF, 0)
        k_rows = lax.dynamic_slice_in_dim(keys, start, SUF, 0)
        v_rows = lax.dynamic_slice_in_dim(vals, start, SUF, 0)
        length = suffix_len[index]
        pages = page_table[request_group[index]]
        prefix_keys = jnp.take(key_pool, pages, axis=0).reshape(PPG * PAGE, KVH, HD)
        prefix_vals = jnp.take(value_pool, pages, axis=0).reshape(PPG * PAGE, KVH, HD)
        first = partial_attention(q_rows, prefix_keys, prefix_vals, None)
        rows = jnp.arange(SUF, dtype=jnp.int32)
        mask = (rows[None, :] <= rows[:, None]) & (rows[None, :] < length)
        second = partial_attention(q_rows, k_rows, v_rows, mask)
        top, total, out = combine(first, second)
        valid = (rows < length).astype(jnp.float32)
        return out / total[..., None] * valid[:, None, None, None]
    attention = lax.map(one_request, jnp.arange(REQUESTS, dtype=jnp.int32)).reshape(TOKENS, TOPK, KVH * HD)
    weighted = (gates[:, :, None] * attention).astype(jnp.bfloat16)
    result = jnp.zeros((TOKENS, D), jnp.float32)
    for expert in range(EXPERTS):
        picked = jnp.zeros((TOKENS, KVH * HD), jnp.bfloat16)
        for slot in range(TOPK):
            picked = jnp.where(att_experts[:, slot:slot + 1] == expert, weighted[:, slot], picked)
        result = result + jnp.dot(picked, w_out[expert], preferred_element_type=jnp.float32)
    return result.astype(jnp.bfloat16)
```

```python
import functools

import jax
import jax.numpy as jnp
import numpy as np
from jax import lax
from jax.experimental import pallas as pl
from jax.experimental.pallas import tpu as pltpu
from jax.sharding import PartitionSpec as P

HD = 128
F32 = jnp.float32
BF16 = jnp.bfloat16
NEG = -1e30
NBUF = 4
MESH = pl.DeviceIdType.MESH


def rope_tables(rows, first):
    half = HD // 2
    freq = (10000.0 ** (-np.arange(half, dtype=np.float64) * 2.0 / HD)).astype(np.float32)
    angle = (np.arange(rows, dtype=np.float32)[:, None] + np.float32(first)) * freq[None, :]
    cosine, sine = np.cos(angle), np.sin(angle)
    return (
        np.concatenate([cosine, cosine], axis=1).astype(np.float32),
        np.concatenate([-sine, sine], axis=1).astype(np.float32),
    )


def project_kernel(
    hidden, gain, router, att, cos, sin, wq, wk, wv,
    q_out, k_out, vt_out, gate_out,
    wbuf, kvbuf, normed, qacc, sems, kvsems,
):
    experts, _, cols = wq.shape
    heads = cols // HD
    rows = hidden.shape[0]
    topk = att.shape[1]

    def fetch(e, slot):
        return pltpu.make_async_copy(wq.at[e], wbuf.at[slot], sems.at[slot])

    for e in range(NBUF):
        fetch(e, e).start()
    fetch_k = pltpu.make_async_copy(wk, kvbuf.at[0], kvsems.at[0])
    fetch_v = pltpu.make_async_copy(wv, kvbuf.at[1], kvsems.at[1])
    fetch_k.start()
    fetch_v.start()

    state = hidden[...].astype(F32)
    inv = lax.rsqrt(jnp.mean(state * state, axis=-1, keepdims=True) + 1e-06)
    normed[...] = (state * inv * gain[...]).astype(BF16)
    logits = jnp.dot(normed[...], router[...], preferred_element_type=F32)
    lane = lax.broadcasted_iota(jnp.int32, logits.shape, 1)
    picks = [
        jnp.sum(jnp.where(lane == att[:, s : s + 1], logits, 0.0), axis=1, keepdims=True)
        for s in range(topk)
    ]
    top = functools.reduce(jnp.maximum, picks)
    raised = [jnp.exp(x - top) for x in picks]
    total = functools.reduce(jnp.add, raised)
    for s in range(topk):
        gate_out[s * rows : (s + 1) * rows, :] = raised[s] / total
    qacc[...] = jnp.zeros_like(qacc)

    def step(e, carry):
        slot = lax.rem(e, NBUF)
        fetch(e, slot).wait()
        prod = jnp.dot(normed[...], wbuf[slot], preferred_element_type=F32)
        for s in range(topk):
            qacc[s] = jnp.where(att[:, s : s + 1] == e, prod, qacc[s])

        @pl.when(e + NBUF < experts)
        def _():
            fetch(e + NBUF, slot).start()

        return carry

    lax.fori_loop(0, experts, step, 0)

    def rope(u):
        return u * cos[...] + pltpu.roll(u, HD // 2, 1) * sin[...]

    for h in range(heads):
        for s in range(topk):
            q_out[h, s * rows : (s + 1) * rows, :] = rope(
                qacc[s, :, h * HD : (h + 1) * HD]
            ).astype(BF16)
    fetch_k.wait()
    keys = jnp.dot(normed[...], kvbuf[0], preferred_element_type=F32)
    for h in range(heads):
        k_out[h] = rope(keys[:, h * HD : (h + 1) * HD]).astype(BF16)
    fetch_v.wait()
    vals = jnp.dot(normed[...], kvbuf[1], preferred_element_type=F32)
    for h in range(heads):
        vt_out[h] = vals[:, h * HD : (h + 1) * HD].T.astype(BF16)


def attend_kernel(
    tok_bits, head_bits, units,
    meta, length, q_in, k_in, vt_in, gates, att, kpool, vpool, wout,
    out,
    *scratch,
):
    heads, qrows, _ = q_in.shape
    suffix = k_in.shape[1]
    topk = qrows // suffix
    pages = kpool.shape[0]
    rounds = len(tok_bits)
    half = 2 ** (rounds - 1)
    experts = wout.shape[0] // (heads * HD)
    scale = 1.0 / HD**0.5
    blocks = 2 ** len(head_bits)
    width = wout.shape[1] // blocks

    it = iter(scratch)
    qall = [next(it) for _ in range(heads)]
    sbuf = [[next(it) for _ in range(rounds)] for _ in range(heads)]
    sstat = [[next(it) for _ in range(rounds)] for _ in range(heads)]
    rbuf = [[next(it) for _ in range(rounds)] for _ in range(heads)]
    rstat = [[next(it) for _ in range(rounds)] for _ in range(heads)]
    vt = next(it)
    ust = next(it)
    ustat = next(it)
    cur = next(it)
    cstat = next(it)
    wbuf = next(it)
    picked = next(it)
    osend = [next(it) for _ in head_bits]
    orecv = [next(it) for _ in head_bits]
    oacc = next(it)
    ag_s, ag_r = next(it), next(it)
    rs_s, rs_r = next(it), next(it)
    rt_s, rt_r = next(it), next(it)
    o_s, o_r = next(it), next(it)
    w_sem = next(it)
    q_sem = next(it)

    tok = lax.axis_index("tok")
    head = lax.axis_index("head")

    def flip(index, bit):
        return index + bit * (1 - 2 * ((index // bit) % 2))

    partners = [{"tok": flip(tok, b)} for b in tok_bits]
    mates = [{"head": flip(head, b)} for b in head_bits]

    barrier = pltpu.get_barrier_semaphore()
    for other in partners + mates:
        pl.semaphore_signal(barrier, inc=1, device_id=other, device_id_type=MESH)

    def block_of(j):
        col = head
        for n, b in enumerate(head_bits):
            if (j >> n) & 1:
                col = flip(col, b)
        return col

    local_q = []
    for h in range(heads):
        c = pltpu.make_async_copy(q_in.at[h], qall[h].at[0], q_sem.at[h])
        c.start()
        local_q.append(c)
    loads = []
    for j in range(blocks):
        c = pltpu.make_async_copy(
            wout.at[:, pl.ds(pl.multiple_of(block_of(j) * width, 128), width)],
            wbuf.at[j],
            w_sem.at[j],
        )
        c.start()
        loads.append(c)
    pl.semaphore_wait(barrier, len(partners) + len(mates))

    def gather_copy(h, k):
        n = 2**k
        return pltpu.make_async_remote_copy(
            src_ref=qall[h].at[pl.ds(0, n)],
            dst_ref=qall[h].at[pl.ds(n, n)],
            send_sem=ag_s.at[h, k],
            recv_sem=ag_r.at[h, k],
            device_id=partners[k],
            device_id_type=MESH,
        )

    for h in range(heads):
        local_q[h].wait()
        gather_copy(h, 0).start()
    for p in range(pages):
        for h in range(heads):
            vt[h, p] = vpool[p, :, h * HD : (h + 1) * HD].T
    ust[0] = jnp.zeros_like(ust[0])
    ustat[0, 0:1] = jnp.full((1, qrows), NEG, F32)
    ustat[0, 1:2] = jnp.zeros((1, qrows), F32)
    for k in range(1, rounds):
        for h in range(heads):
            gather_copy(h, k - 1).wait_recv()
            gather_copy(h, k).start()

    def scores_t(keys, queries):
        return (
            lax.dot_general(
                keys, queries, (((1,), (1,)), ((), ())), preferred_element_type=F32
            )
            * scale
        )

    def attend(h):
        def unit(u, carry):
            req, page, same = meta[0, u], meta[1, u], meta[2, u]
            s = scores_t(kpool[page, :, h * HD : (h + 1) * HD], qall[h][req])
            m_old = jnp.where(same == 1, ustat[u, 0:1], NEG)
            m_new = jnp.maximum(m_old, jnp.max(s, axis=0, keepdims=True))
            alpha = jnp.exp(m_old - m_new)
            w = jnp.exp(s - m_new)
            ustat[u + 1, 0:1] = m_new
            ustat[u + 1, 1:2] = ustat[u, 1:2] * alpha + jnp.sum(w, axis=0, keepdims=True)
            ust[u + 1] = ust[u] * alpha + jnp.dot(
                vt[h, page], w.astype(BF16), preferred_element_type=F32
            )
            return carry

        lax.fori_loop(0, units, unit, 0)

        def keep(i, carry):
            cur[h, i] = ust[meta[3, i]]
            cstat[h, i] = ustat[meta[3, i]]
            return carry

        lax.fori_loop(0, half, keep, 0)

        def give(i, carry):
            sbuf[h][0][i] = ust[meta[3, half + i]].astype(BF16)
            sstat[h][0][i] = ustat[meta[3, half + i]]
            return carry

        lax.fori_loop(0, half, give, 0)

    def reduce_copies(h, k):
        bit = rounds - 1 - k
        return (
            pltpu.make_async_remote_copy(
                src_ref=sbuf[h][k], dst_ref=rbuf[h][k],
                send_sem=rs_s.at[h, k], recv_sem=rs_r.at[h, k],
                device_id=partners[bit], device_id_type=MESH,
            ),
            pltpu.make_async_remote_copy(
                src_ref=sstat[h][k], dst_ref=rstat[h][k],
                send_sem=rt_s.at[h, k], recv_sem=rt_r.at[h, k],
                device_id=partners[bit], device_id_type=MESH,
            ),
        )

    def merged(m_a, l_a, o_a, m_b, l_b, o_b):
        m = jnp.maximum(m_a, m_b)
        a, b = jnp.exp(m_a - m), jnp.exp(m_b - m)
        return m, l_a * a + l_b * b, o_a * a + o_b * b

    def merge_at(h, k, i):
        return merged(
            cstat[h, i, 0:1], cstat[h, i, 1:2], cur[h, i],
            rstat[h][k][i, 0:1], rstat[h][k][i, 1:2], rbuf[h][k][i].astype(F32),
        )

    for h in range(heads):
        gather_copy(h, rounds - 1).wait_recv()
        attend(h)
        for c in reduce_copies(h, 0):
            c.start()

    slot = lax.broadcasted_iota(jnp.int32, (suffix, qrows), 1) % suffix
    key_at = lax.broadcasted_iota(jnp.int32, (suffix, qrows), 0)
    mask = (key_at <= slot) & (key_at < length[0])

    for k in range(rounds - 1):
        n = 2 ** (rounds - 2 - k)
        for h in range(heads):
            for c in reduce_copies(h, k):
                c.wait_recv()

            def give(i, carry, h=h, k=k, n=n):
                m, l, o = merge_at(h, k, n + i)
                sstat[h][k + 1][i, 0:1] = m
                sstat[h][k + 1][i, 1:2] = l
                sbuf[h][k + 1][i] = o.astype(BF16)
                return carry

            lax.fori_loop(0, n, give, 0)
            for c in reduce_copies(h, k + 1):
                c.start()

            def keep(i, carry, h=h, k=k):
                m, l, o = merge_at(h, k, i)
                cstat[h, i, 0:1] = m
                cstat[h, i, 1:2] = l
                cur[h, i] = o
                return carry

            lax.fori_loop(0, n, keep, 0)
            if k == 0:
                s = jnp.where(mask, scores_t(k_in[h], q_in[h]), NEG)
                m_s = jnp.max(s, axis=0, keepdims=True)
                w = jnp.exp(s - m_s)
                l_s = jnp.sum(w, axis=0, keepdims=True)
                o_s_ = jnp.dot(vt_in[h], w.astype(BF16), preferred_element_type=F32)
                m, l, o = merged(
                    cstat[h, 0, 0:1], cstat[h, 0, 1:2], cur[h, 0], m_s, l_s, o_s_
                )
                cstat[h, 0, 0:1] = m
                cstat[h, 0, 1:2] = l
                cur[h, 0] = o

    row = lax.broadcasted_iota(jnp.int32, (qrows, 1), 0) % suffix
    factor = gates[...] * (row < length[0]).astype(F32)
    for h in range(heads):
        for c in reduce_copies(h, rounds - 1):
            c.wait_recv()
        m, l, o = merge_at(h, rounds - 1, 0)
        weighted = ((o / l).T * factor).astype(F32)
        for e in range(experts):
            value = jnp.zeros((suffix, HD), F32)
            for s in range(topk):
                value = jnp.where(
                    att[:, s : s + 1] == e, weighted[s * suffix : (s + 1) * suffix], value
                )
            picked[:, (e * heads + h) * HD : (e * heads + h + 1) * HD] = value.astype(BF16)

    depth = heads * HD

    def multiply(j):
        loads[j].wait()
        oacc[...] = jnp.zeros_like(oacc)

        def part(e, carry):
            at = pl.ds(pl.multiple_of(e * depth, depth), depth)
            oacc[...] += jnp.dot(picked[:, at], wbuf[j, at, :], preferred_element_type=F32)
            return carry

        lax.fori_loop(0, experts, part, 0)
        return oacc[...]

    def out_copy(k):
        return pltpu.make_async_remote_copy(
            src_ref=osend[k], dst_ref=orecv[k],
            send_sem=o_s.at[k], recv_sem=o_r.at[k],
            device_id=mates[len(head_bits) - 1 - k], device_id_type=MESH,
        )

    levels = len(head_bits)
    for j in range(blocks // 2, blocks):
        osend[0][j - blocks // 2] = multiply(j).astype(BF16)
    out_copy(0).start()
    for k in range(1, levels):
        n = 2 ** (levels - 1 - k)
        own = [multiply(j) for j in range(n, 2 * n)]
        out_copy(k - 1).wait_recv()
        for j in range(n):
            total = own[j]
            for i in range(k):
                total = total + orecv[i][n + j].astype(F32)
            osend[k][j] = total.astype(BF16)
        out_copy(k).start()
    total = multiply(0)
    out_copy(levels - 1).wait_recv()
    for i in range(levels):
        total = total + orecv[i][0].astype(F32)
    out[...] = total.astype(BF16)

    for k in range(levels):
        out_copy(k).wait_send()
    for h in range(heads):
        for k in range(rounds):
            gather_copy(h, k).wait_send()
            for c in reduce_copies(h, k):
                c.wait_send()


def unit_table(page_table, request_group, deltas, local_pages):
    groups, per_group = page_table.shape
    requests = request_group.shape[0]
    units = local_pages * (requests // groups)
    tok = lax.axis_index("tok")
    order = jnp.bitwise_xor(tok, jnp.asarray(deltas, jnp.int32))
    number = jnp.arange(requests, dtype=jnp.int32)
    group_of = jnp.sum(
        jnp.where(order[:, None] == number[None, :], request_group[None, :], 0), axis=1
    )
    mine = tok * local_pages + jnp.arange(local_pages, dtype=jnp.int32)
    flat = page_table.reshape(-1)
    owner = jnp.arange(flat.shape[0], dtype=jnp.int32) // per_group
    page_group = jnp.sum(jnp.where(flat[None, :] == mine[:, None], owner[None, :], 0), axis=1)
    uses = (group_of[:, None] == page_group[None, :]).astype(jnp.int32).reshape(-1)
    count = uses.shape[0]
    place = jnp.arange(count, dtype=jnp.int32)
    running = jnp.sum(jnp.where(place[None, :] <= place[:, None], uses[None, :], 0), axis=1)
    at = jnp.sum(
        (running[None, :] <= jnp.arange(units, dtype=jnp.int32)[:, None]).astype(jnp.int32), axis=1
    )
    req, page = at // local_pages, at % local_pages
    before = jnp.concatenate([jnp.full((1,), -1, jnp.int32), req[:-1]])
    per = uses.reshape(requests, local_pages)
    ends = running.reshape(requests, local_pages)[:, -1]
    last = jnp.where(jnp.sum(per, axis=1) > 0, ends, 0)
    size = max(units, requests)
    pad = lambda x: jnp.pad(x, (0, size - x.shape[0]))
    return jnp.stack([pad(req), pad(page), pad((req == before).astype(jnp.int32)), pad(last)])


def per_device(
    toks, heads_dev,
    hidden, norm_gain, w_router, w_query, w_key, w_value, w_out,
    key_pool, value_pool, page_table, request_group, suffix_len, att_experts,
):
    rows, model = hidden.shape
    cols = w_key.shape[1]
    heads = cols // HD
    topk = att_experts.shape[1]
    experts = w_query.shape[0]
    prefix = page_table.shape[1] * key_pool.shape[1]
    pages = key_pool.shape[0]
    requests = request_group.shape[0]
    page_rows = key_pool.shape[1]
    qrows = topk * rows
    x = max(toks // 4, 1)
    bits = [1 << n for n in range(toks.bit_length() - 1)]
    tok_bits = [b for b in bits if b >= x] + [b for b in bits if b < x]
    rounds = len(tok_bits)
    deltas = [
        sum(b for n, b in enumerate(tok_bits) if (i >> n) & 1) for i in range(toks)
    ]
    head_bits = [1 << n for n in range(1, heads_dev.bit_length() - 1)] + [1]
    levels = len(head_bits)
    units = pages * (requests // page_table.shape[0])
    meta = unit_table(page_table, request_group, deltas, pages)
    cos, sin = rope_tables(rows, prefix)
    vm = pl.BlockSpec(memory_space=pltpu.VMEM)
    sm = pl.BlockSpec(memory_space=pltpu.SMEM)
    hbm = pl.BlockSpec(memory_space=pl.ANY)
    q, k, vt, gates = pl.pallas_call(
        project_kernel,
        out_shape=(
            jax.ShapeDtypeStruct((heads, qrows, HD), BF16),
            jax.ShapeDtypeStruct((heads, rows, HD), BF16),
            jax.ShapeDtypeStruct((heads, HD, rows), BF16),
            jax.ShapeDtypeStruct((qrows, 1), F32),
        ),
        in_specs=[vm] * 6 + [hbm] * 3,
        out_specs=(vm,) * 4,
        scratch_shapes=[
            pltpu.VMEM((NBUF, model, cols), BF16),
            pltpu.VMEM((2, model, cols), BF16),
            pltpu.VMEM((rows, model), BF16),
            pltpu.VMEM((topk, rows, cols), F32),
            pltpu.SemaphoreType.DMA((NBUF,)),
            pltpu.SemaphoreType.DMA((2,)),
        ],
        compiler_params=pltpu.CompilerParams(vmem_limit_bytes=40 * 2**20),
        name="project",
    )(
        hidden, norm_gain.reshape(1, -1), w_router, att_experts,
        jnp.asarray(cos), jnp.asarray(sin), w_query, w_key, w_value,
    )
    sizes = [2 ** (rounds - 1 - k_) for k_ in range(rounds)]
    width = model // heads_dev
    dma = pltpu.SemaphoreType.DMA
    scratch = (
        [pltpu.VMEM((toks, qrows, HD), BF16) for _ in range(heads)]
        + [pltpu.VMEM((n, HD, qrows), BF16) for _ in range(heads) for n in sizes]
        + [pltpu.VMEM((n, 2, qrows), F32) for _ in range(heads) for n in sizes]
        + [pltpu.VMEM((n, HD, qrows), BF16) for _ in range(heads) for n in sizes]
        + [pltpu.VMEM((n, 2, qrows), F32) for _ in range(heads) for n in sizes]
        + [
            pltpu.VMEM((heads, pages, HD, page_rows), BF16),
            pltpu.VMEM((units + 1, HD, qrows), F32),
            pltpu.VMEM((units + 1, 2, qrows), F32),
            pltpu.VMEM((heads, sizes[0], HD, qrows), F32),
            pltpu.VMEM((heads, sizes[0], 2, qrows), F32),
            pltpu.VMEM((heads_dev, experts * cols, width), BF16),
            pltpu.VMEM((rows, experts * cols), BF16),
        ]
        + [pltpu.VMEM((2 ** (levels - 1 - k_), rows, width), BF16) for k_ in range(levels)] * 2
        + [
            pltpu.VMEM((rows, width), F32),
            dma((heads, rounds)), dma((heads, rounds)),
            dma((heads, rounds)), dma((heads, rounds)),
            dma((heads, rounds)), dma((heads, rounds)),
            dma((levels,)), dma((levels,)),
            dma((heads_dev,)), dma((heads,)),
        ]
    )
    return pl.pallas_call(
        functools.partial(attend_kernel, tok_bits, head_bits, units),
        out_shape=jax.ShapeDtypeStruct((rows, width), BF16),
        in_specs=[sm, sm] + [vm] * 7 + [hbm],
        out_specs=vm,
        scratch_shapes=scratch,
        compiler_params=pltpu.CompilerParams(
            collective_id=0, has_side_effects=True, vmem_limit_bytes=56 * 2**20
        ),
        name="attend",
    )(
        meta, suffix_len, q, k, vt, gates, att_experts, key_pool, value_pool,
        w_out.reshape(experts * cols, model),
    )


def solution(mesh):
    return jax.shard_map(
        functools.partial(per_device, mesh.shape["tok"], mesh.shape["head"]),
        mesh=mesh,
        in_specs=(
            P("tok", None), P(), P(), P(None, None, "head"), P(None, "head"), P(None, "head"),
            P(None, "head", None), P("tok", None, "head"), P("tok", None, "head"),
            P(), P(), P("tok"), P("tok", None),
        ),
        out_specs=P("tok", "head"),
        check_vma=False,
    )
```

```python
import functools

import jax
import jax.numpy as jnp
import numpy as np
from jax import lax
from jax.experimental import pallas as pl
from jax.experimental.pallas import tpu as pltpu
from jax.sharding import PartitionSpec as P

HD = 128
F32 = jnp.float32
BF16 = jnp.bfloat16
NEG = -1e30
MESH = pl.DeviceIdType.MESH


def rope_tables(rows, first):
    half = HD // 2
    freq = (10000.0 ** (-np.arange(half, dtype=np.float64) * 2.0 / HD)).astype(np.float32)
    angle = (np.arange(rows, dtype=np.float32)[:, None] + np.float32(first)) * freq[None, :]
    cosine, sine = np.cos(angle), np.sin(angle)
    return (
        np.concatenate([cosine, cosine], axis=1).astype(np.float32),
        np.concatenate([-sine, sine], axis=1).astype(np.float32),
    )


def attend_kernel(
    tok_bits, head_bits, units,
    meta, length, hidden, gain, router, att, cos, sin, kpool, vpool, wq, wk, wv, wout,
    out,
    *scratch,
):
    suffix = hidden.shape[0]
    topk = att.shape[1]
    qrows = topk * suffix
    heads = wk.shape[1] // HD
    pages = kpool.shape[0]
    rounds = len(tok_bits)
    half = 2 ** (rounds - 1)
    experts = wout.shape[0] // (heads * HD)
    scale = 1.0 / HD**0.5
    blocks = 2 ** len(head_bits)
    width = wout.shape[1] // blocks

    it = iter(scratch)
    qall = [next(it) for _ in range(heads)]
    sbuf = [[next(it) for _ in range(rounds)] for _ in range(heads)]
    sstat = [[next(it) for _ in range(rounds)] for _ in range(heads)]
    rbuf = [[next(it) for _ in range(rounds)] for _ in range(heads)]
    rstat = [[next(it) for _ in range(rounds)] for _ in range(heads)]
    vt = next(it)
    ust = next(it)
    ustat = next(it)
    cur = next(it)
    cstat = next(it)
    wbuf = next(it)
    picked = next(it)
    osend = [next(it) for _ in head_bits]
    orecv = [next(it) for _ in head_bits]
    oacc = next(it)
    ag_s, ag_r = next(it), next(it)
    rs_s, rs_r = next(it), next(it)
    rt_s, rt_r = next(it), next(it)
    o_s, o_r = next(it), next(it)
    w_sem = next(it)
    q_sem = next(it)
    kv_sem = next(it)
    wqbuf, kvbuf, normed, qacc, k_in, vt_in, gates = [next(it) for _ in range(7)]

    tok = lax.axis_index("tok")
    head = lax.axis_index("head")

    def flip(index, bit):
        return index + bit * (1 - 2 * ((index // bit) % 2))

    partners = [{"tok": flip(tok, b)} for b in tok_bits]
    mates = [{"head": flip(head, b)} for b in head_bits]

    barrier = pltpu.get_barrier_semaphore()
    for other in partners + mates:
        pl.semaphore_signal(barrier, inc=1, device_id=other, device_id_type=MESH)

    def block_of(j):
        col = head
        for n, b in enumerate(head_bits):
            if (j >> n) & 1:
                col = flip(col, b)
        return col

    def fetch_q(h):
        return pltpu.make_async_copy(
            wq.at[:, :, pl.ds(h * HD, HD)], wqbuf.at[h % 2], q_sem.at[h % 2]
        )

    fetch_k = pltpu.make_async_copy(wk, kvbuf.at[0], kv_sem.at[0])
    fetch_v = pltpu.make_async_copy(wv, kvbuf.at[1], kv_sem.at[1])
    loads = [
        pltpu.make_async_copy(
            wout.at[:, pl.ds(pl.multiple_of(block_of(j) * width, 128), width)],
            wbuf.at[j],
            w_sem.at[j],
        )
        for j in range(blocks)
    ]
    for h in range(min(2, heads)):
        fetch_q(h).start()

    state = hidden[...].astype(F32)
    inv = lax.rsqrt(jnp.mean(state * state, axis=-1, keepdims=True) + 1e-06)
    normed[...] = (state * inv * gain[...]).astype(BF16)

    def rope(u):
        return u * cos[...] + pltpu.roll(u, HD // 2, 1) * sin[...]

    def project(h):
        fetch_q(h).wait()
        qacc[...] = jnp.zeros_like(qacc)

        def step(e, carry):
            prod = jnp.dot(normed[...], wqbuf[h % 2, e], preferred_element_type=F32)
            for s in range(topk):
                qacc[s] = jnp.where(att[:, s : s + 1] == e, prod, qacc[s])
            return carry

        lax.fori_loop(0, experts, step, 0)
        if h + 2 < heads:
            fetch_q(h + 2).start()
        for s in range(topk):
            qall[h][0, s * suffix : (s + 1) * suffix, :] = rope(qacc[s]).astype(BF16)

    def project_keys():
        fetch_k.wait()
        keys = jnp.dot(normed[...], kvbuf[0], preferred_element_type=F32)
        for h in range(heads):
            k_in[h] = rope(keys[:, h * HD : (h + 1) * HD]).astype(BF16)

    def project_values():
        fetch_v.wait()
        vals = jnp.dot(normed[...], kvbuf[1], preferred_element_type=F32)
        for h in range(heads):
            vt_in[h] = vals[:, h * HD : (h + 1) * HD].T.astype(BF16)

    def route():
        logits = jnp.dot(normed[...], router[...], preferred_element_type=F32)
        lane = lax.broadcasted_iota(jnp.int32, logits.shape, 1)
        picks = [
            jnp.sum(jnp.where(lane == att[:, s : s + 1], logits, 0.0), axis=1, keepdims=True)
            for s in range(topk)
        ]
        top = functools.reduce(jnp.maximum, picks)
        raised = [jnp.exp(x - top) for x in picks]
        total = functools.reduce(jnp.add, raised)
        for s in range(topk):
            gates[s * suffix : (s + 1) * suffix, :] = raised[s] / total

    pl.semaphore_wait(barrier, len(partners) + len(mates))

    def gather_copy(h, k):
        n = 2**k
        return pltpu.make_async_remote_copy(
            src_ref=qall[h].at[pl.ds(0, n)],
            dst_ref=qall[h].at[pl.ds(n, n)],
            send_sem=ag_s.at[h, k],
            recv_sem=ag_r.at[h, k],
            device_id=partners[k],
            device_id_type=MESH,
        )

    ust[0] = jnp.zeros_like(ust[0])
    ustat[0, 0:1] = jnp.full((1, qrows), NEG, F32)
    ustat[0, 1:2] = jnp.zeros((1, qrows), F32)

    def scores_t(keys, queries):
        return (
            lax.dot_general(
                keys, queries, (((1,), (1,)), ((), ())), preferred_element_type=F32
            )
            * scale
        )

    def attend(h):
        def unit(u, carry):
            req, page, same = meta[0, u], meta[1, u], meta[2, u]
            s = scores_t(kpool[page, :, h * HD : (h + 1) * HD], qall[h][req])
            m_old = jnp.where(same == 1, ustat[u, 0:1], NEG)
            m_new = jnp.maximum(m_old, jnp.max(s, axis=0, keepdims=True))
            alpha = jnp.exp(m_old - m_new)
            w = jnp.exp(s - m_new)
            ustat[u + 1, 0:1] = m_new
            ustat[u + 1, 1:2] = ustat[u, 1:2] * alpha + jnp.sum(w, axis=0, keepdims=True)
            ust[u + 1] = ust[u] * alpha + jnp.dot(
                vt[h, page], w.astype(BF16), preferred_element_type=F32
            )
            return carry

        lax.fori_loop(0, units, unit, 0)

        def keep(i, carry):
            cur[h, i] = ust[meta[3, i]]
            cstat[h, i] = ustat[meta[3, i]]
            return carry

        lax.fori_loop(0, half, keep, 0)

        def give(i, carry):
            sbuf[h][0][i] = ust[meta[3, half + i]].astype(BF16)
            sstat[h][0][i] = ustat[meta[3, half + i]]
            return carry

        lax.fori_loop(0, half, give, 0)

    def reduce_copies(h, k):
        bit = rounds - 1 - k
        return (
            pltpu.make_async_remote_copy(
                src_ref=sbuf[h][k], dst_ref=rbuf[h][k],
                send_sem=rs_s.at[h, k], recv_sem=rs_r.at[h, k],
                device_id=partners[bit], device_id_type=MESH,
            ),
            pltpu.make_async_remote_copy(
                src_ref=sstat[h][k], dst_ref=rstat[h][k],
                send_sem=rt_s.at[h, k], recv_sem=rt_r.at[h, k],
                device_id=partners[bit], device_id_type=MESH,
            ),
        )

    def merged(m_a, l_a, o_a, m_b, l_b, o_b):
        m = jnp.maximum(m_a, m_b)
        a, b = jnp.exp(m_a - m), jnp.exp(m_b - m)
        return m, l_a * a + l_b * b, o_a * a + o_b * b

    def merge_at(h, k, i):
        return merged(
            cstat[h, i, 0:1], cstat[h, i, 1:2], cur[h, i],
            rstat[h][k][i, 0:1], rstat[h][k][i, 1:2], rbuf[h][k][i].astype(F32),
        )

    slot = lax.broadcasted_iota(jnp.int32, (suffix, qrows), 1) % suffix
    key_at = lax.broadcasted_iota(jnp.int32, (suffix, qrows), 0)
    mask = (key_at <= slot) & (key_at < length[0])

    def pass_on(h, k):
        n = 2 ** (rounds - 2 - k)
        for c in reduce_copies(h, k):
            c.wait_recv()

        def give(i, carry, h=h, k=k, n=n):
            m, l, o = merge_at(h, k, n + i)
            sstat[h][k + 1][i, 0:1] = m
            sstat[h][k + 1][i, 1:2] = l
            sbuf[h][k + 1][i] = o.astype(BF16)
            return carry

        lax.fori_loop(0, n, give, 0)
        for c in reduce_copies(h, k + 1):
            c.start()

        def keep(i, carry, h=h, k=k):
            m, l, o = merge_at(h, k, i)
            cstat[h, i, 0:1] = m
            cstat[h, i, 1:2] = l
            cur[h, i] = o
            return carry

        lax.fori_loop(0, n, keep, 0)
        if k == 0:
            s = jnp.where(mask, scores_t(k_in[h], qall[h][0]), NEG)
            m_s = jnp.max(s, axis=0, keepdims=True)
            w = jnp.exp(s - m_s)
            l_s = jnp.sum(w, axis=0, keepdims=True)
            o_s_ = jnp.dot(vt_in[h], w.astype(BF16), preferred_element_type=F32)
            m, l, o = merged(
                cstat[h, 0, 0:1], cstat[h, 0, 1:2], cur[h, 0], m_s, l_s, o_s_
            )
            cstat[h, 0, 0:1] = m
            cstat[h, 0, 1:2] = l
            cur[h, 0] = o


    for t in range(heads + 2 * rounds - 1):
        for k in range(rounds, -1, -1):
            h = t - k
            if 0 <= h < heads:
                if k > 0:
                    gather_copy(h, k - 1).wait_recv()
                if k < rounds:
                    if k == 0:
                        project(h)
                    gather_copy(h, k).start()
        if t == 0:
            fetch_k.start()
            fetch_v.start()
        if t == 1:
            project_keys()
        if t == 2:
            project_values()
            route()
        if t == max(heads - 1, 2):
            for c in loads:
                c.start()
        if t < heads:
            for p in range(pages):
                vt[t, p] = vpool[p, :, t * HD : (t + 1) * HD].T
        for k in range(rounds - 2, -1, -1):
            h = t - rounds - 1 - k
            if 0 <= h < heads:
                pass_on(h, k)
        if 0 <= t - rounds < heads:
            attend(t - rounds)
            for c in reduce_copies(t - rounds, 0):
                c.start()

    row = lax.broadcasted_iota(jnp.int32, (qrows, 1), 0) % suffix
    factor = gates[...] * (row < length[0]).astype(F32)
    for h in range(heads):
        for c in reduce_copies(h, rounds - 1):
            c.wait_recv()
        m, l, o = merge_at(h, rounds - 1, 0)
        weighted = ((o / l).T * factor).astype(F32)
        for e in range(experts):
            value = jnp.zeros((suffix, HD), F32)
            for s in range(topk):
                value = jnp.where(
                    att[:, s : s + 1] == e, weighted[s * suffix : (s + 1) * suffix], value
                )
            picked[:, (e * heads + h) * HD : (e * heads + h + 1) * HD] = value.astype(BF16)

    depth = heads * HD

    def multiply(j):
        loads[j].wait()
        oacc[...] = jnp.zeros_like(oacc)

        def part(e, carry):
            at = pl.ds(pl.multiple_of(e * depth, depth), depth)
            oacc[...] += jnp.dot(picked[:, at], wbuf[j, at, :], preferred_element_type=F32)
            return carry

        lax.fori_loop(0, experts, part, 0)
        return oacc[...]

    def out_copy(k):
        return pltpu.make_async_remote_copy(
            src_ref=osend[k], dst_ref=orecv[k],
            send_sem=o_s.at[k], recv_sem=o_r.at[k],
            device_id=mates[len(head_bits) - 1 - k], device_id_type=MESH,
        )

    levels = len(head_bits)
    for j in range(blocks // 2, blocks):
        osend[0][j - blocks // 2] = multiply(j).astype(BF16)
    out_copy(0).start()
    for k in range(1, levels):
        n = 2 ** (levels - 1 - k)
        own = [multiply(j) for j in range(n, 2 * n)]
        out_copy(k - 1).wait_recv()
        for j in range(n):
            total = own[j]
            for i in range(k):
                total = total + orecv[i][n + j].astype(F32)
            osend[k][j] = total.astype(BF16)
        out_copy(k).start()
    total = multiply(0)
    out_copy(levels - 1).wait_recv()
    for i in range(levels):
        total = total + orecv[i][0].astype(F32)
    out[...] = total.astype(BF16)

    for k in range(levels):
        out_copy(k).wait_send()
    for h in range(heads):
        for k in range(rounds):
            gather_copy(h, k).wait_send()
            for c in reduce_copies(h, k):
                c.wait_send()


def unit_table(page_table, request_group, deltas, local_pages):
    groups, per_group = page_table.shape
    requests = request_group.shape[0]
    units = local_pages * (requests // groups)
    tok = lax.axis_index("tok")
    order = jnp.bitwise_xor(tok, jnp.asarray(deltas, jnp.int32))
    number = jnp.arange(requests, dtype=jnp.int32)
    group_of = jnp.sum(
        jnp.where(order[:, None] == number[None, :], request_group[None, :], 0), axis=1
    )
    mine = tok * local_pages + jnp.arange(local_pages, dtype=jnp.int32)
    flat = page_table.reshape(-1)
    owner = jnp.arange(flat.shape[0], dtype=jnp.int32) // per_group
    page_group = jnp.sum(jnp.where(flat[None, :] == mine[:, None], owner[None, :], 0), axis=1)
    uses = (group_of[:, None] == page_group[None, :]).astype(jnp.int32).reshape(-1)
    count = uses.shape[0]
    place = jnp.arange(count, dtype=jnp.int32)
    running = jnp.sum(jnp.where(place[None, :] <= place[:, None], uses[None, :], 0), axis=1)
    at = jnp.sum(
        (running[None, :] <= jnp.arange(units, dtype=jnp.int32)[:, None]).astype(jnp.int32), axis=1
    )
    req, page = at // local_pages, at % local_pages
    before = jnp.concatenate([jnp.full((1,), -1, jnp.int32), req[:-1]])
    per = uses.reshape(requests, local_pages)
    ends = running.reshape(requests, local_pages)[:, -1]
    last = jnp.where(jnp.sum(per, axis=1) > 0, ends, 0)
    size = max(units, requests)
    pad = lambda x: jnp.pad(x, (0, size - x.shape[0]))
    return jnp.stack([pad(req), pad(page), pad((req == before).astype(jnp.int32)), pad(last)])


def per_device(
    toks, heads_dev,
    hidden, norm_gain, w_router, w_query, w_key, w_value, w_out,
    key_pool, value_pool, page_table, request_group, suffix_len, att_experts,
):
    rows, model = hidden.shape
    cols = w_key.shape[1]
    heads = cols // HD
    topk = att_experts.shape[1]
    experts = w_query.shape[0]
    prefix = page_table.shape[1] * key_pool.shape[1]
    pages = key_pool.shape[0]
    requests = request_group.shape[0]
    page_rows = key_pool.shape[1]
    qrows = topk * rows
    x = max(toks // 4, 1)
    bits = [1 << n for n in range(toks.bit_length() - 1)]
    tok_bits = [b for b in bits if b >= x] + [b for b in bits if b < x]
    rounds = len(tok_bits)
    deltas = [
        sum(b for n, b in enumerate(tok_bits) if (i >> n) & 1) for i in range(toks)
    ]
    head_bits = [1 << n for n in range(1, heads_dev.bit_length() - 1)] + [1]
    levels = len(head_bits)
    units = pages * (requests // page_table.shape[0])
    meta = unit_table(page_table, request_group, deltas, pages)
    cos, sin = rope_tables(rows, prefix)
    vm = pl.BlockSpec(memory_space=pltpu.VMEM)
    sm = pl.BlockSpec(memory_space=pltpu.SMEM)
    hbm = pl.BlockSpec(memory_space=pl.ANY)
    sizes = [2 ** (rounds - 1 - k_) for k_ in range(rounds)]
    width = model // heads_dev
    dma = pltpu.SemaphoreType.DMA
    scratch = (
        [pltpu.VMEM((toks, qrows, HD), BF16) for _ in range(heads)]
        + [pltpu.VMEM((n, HD, qrows), BF16) for _ in range(heads) for n in sizes]
        + [pltpu.VMEM((n, 2, qrows), F32) for _ in range(heads) for n in sizes]
        + [pltpu.VMEM((n, HD, qrows), BF16) for _ in range(heads) for n in sizes]
        + [pltpu.VMEM((n, 2, qrows), F32) for _ in range(heads) for n in sizes]
        + [
            pltpu.VMEM((heads, pages, HD, page_rows), BF16),
            pltpu.VMEM((units + 1, HD, qrows), F32),
            pltpu.VMEM((units + 1, 2, qrows), F32),
            pltpu.VMEM((heads, sizes[0], HD, qrows), F32),
            pltpu.VMEM((heads, sizes[0], 2, qrows), F32),
            pltpu.VMEM((heads_dev, experts * cols, width), BF16),
            pltpu.VMEM((rows, experts * cols), BF16),
        ]
        + [pltpu.VMEM((2 ** (levels - 1 - k_), rows, width), BF16) for k_ in range(levels)] * 2
        + [
            pltpu.VMEM((rows, width), F32),
            dma((heads, rounds)), dma((heads, rounds)),
            dma((heads, rounds)), dma((heads, rounds)),
            dma((heads, rounds)), dma((heads, rounds)),
            dma((levels,)), dma((levels,)),
            dma((heads_dev,)), dma((2,)), dma((2,)),
            pltpu.VMEM((2, experts, model, HD), BF16),
            pltpu.VMEM((2, model, cols), BF16),
            pltpu.VMEM((rows, model), BF16),
            pltpu.VMEM((topk, rows, HD), F32),
            pltpu.VMEM((heads, rows, HD), BF16),
            pltpu.VMEM((heads, HD, rows), BF16),
            pltpu.VMEM((qrows, 1), F32),
        ]
    )
    return pl.pallas_call(
        functools.partial(attend_kernel, tok_bits, head_bits, units),
        out_shape=jax.ShapeDtypeStruct((rows, width), BF16),
        in_specs=[sm, sm] + [vm] * 8 + [hbm] * 4,
        out_specs=vm,
        scratch_shapes=scratch,
        compiler_params=pltpu.CompilerParams(
            collective_id=0, has_side_effects=True, vmem_limit_bytes=56 * 2**20
        ),
        name="layer",
    )(
        meta, suffix_len, hidden, norm_gain.reshape(1, -1), w_router, att_experts,
        jnp.asarray(cos), jnp.asarray(sin), key_pool, value_pool, w_query, w_key, w_value,
        w_out.reshape(experts * cols, model),
    )


def solution(mesh):
    return jax.shard_map(
        functools.partial(per_device, mesh.shape["tok"], mesh.shape["head"]),
        mesh=mesh,
        in_specs=(
            P("tok", None), P(), P(), P(None, None, "head"), P(None, "head"), P(None, "head"),
            P(None, "head", None), P("tok", None, "head"), P("tok", None, "head"),
            P(), P(), P("tok"), P("tok", None),
        ),
        out_specs=P("tok", "head"),
        check_vma=False,
    )
```

```python
import functools

import jax
import jax.numpy as jnp
import numpy as np
from jax import lax
from jax.experimental import pallas as pl
from jax.experimental.pallas import tpu as pltpu
from jax.sharding import PartitionSpec as P

HD = 128
F32 = jnp.float32
BF16 = jnp.bfloat16
NEG = -1e30
MESH = pl.DeviceIdType.MESH


def rope_tables(rows, first):
    half = HD // 2
    freq = (10000.0 ** (-np.arange(half, dtype=np.float64) * 2.0 / HD)).astype(np.float32)
    angle = (np.arange(rows, dtype=np.float32)[:, None] + np.float32(first)) * freq[None, :]
    cosine, sine = np.cos(angle), np.sin(angle)
    return (
        np.concatenate([cosine, cosine], axis=1).astype(np.float32),
        np.concatenate([-sine, sine], axis=1).astype(np.float32),
    )


def attend_kernel(
    tok_bits, head_bits, units,
    meta, length, hidden, gain, router, att, cos, sin, kpool, vpool, wq, wk, wv, wout,
    out,
    *scratch,
):
    suffix = hidden.shape[0]
    topk = att.shape[1]
    qrows = topk * suffix
    heads = wk.shape[1] // HD
    pages = kpool.shape[0]
    rounds = len(tok_bits)
    half = 2 ** (rounds - 1)
    experts = wout.shape[0] // (heads * HD)
    scale = 1.0 / HD**0.5
    blocks = 2 ** len(head_bits)
    width = wout.shape[1] // blocks

    it = iter(scratch)
    qall = [next(it) for _ in range(heads)]
    sbuf = [[next(it) for _ in range(rounds)] for _ in range(heads)]
    sstat = [[next(it) for _ in range(rounds)] for _ in range(heads)]
    rbuf = [[next(it) for _ in range(rounds)] for _ in range(heads)]
    rstat = [[next(it) for _ in range(rounds)] for _ in range(heads)]
    vt = next(it)
    ust = next(it)
    ustat = next(it)
    cur = next(it)
    cstat = next(it)
    wbuf = next(it)
    picked = next(it)
    osend = [next(it) for _ in head_bits]
    orecv = [next(it) for _ in head_bits]
    oacc = next(it)
    ag_s, ag_r = next(it), next(it)
    rs_s, rs_r = next(it), next(it)
    rt_s, rt_r = next(it), next(it)
    o_s, o_r = next(it), next(it)
    w_sem = next(it)
    q_sem = next(it)
    kv_sem = next(it)
    wqbuf, kvbuf, normed, qacc, k_in, vt_in, gates = [next(it) for _ in range(7)]

    tok = lax.axis_index("tok")
    head = lax.axis_index("head")

    def flip(index, bit):
        return index + bit * (1 - 2 * ((index // bit) % 2))

    partners = [{"tok": flip(tok, b)} for b in tok_bits]
    mates = [{"head": flip(head, b)} for b in head_bits]

    barrier = pltpu.get_barrier_semaphore()
    for other in partners + mates:
        pl.semaphore_signal(barrier, inc=1, device_id=other, device_id_type=MESH)

    def block_of(j):
        col = head
        for n, b in enumerate(head_bits):
            if (j >> n) & 1:
                col = flip(col, b)
        return col

    def fetch_q(h):
        return pltpu.make_async_copy(
            wq.at[:, :, pl.ds(h * HD, HD)], wqbuf.at[h % 2], q_sem.at[h % 2]
        )

    fetch_k = pltpu.make_async_copy(wk, kvbuf.at[0], kv_sem.at[0])
    fetch_v = pltpu.make_async_copy(wv, kvbuf.at[1], kv_sem.at[1])
    loads = [
        pltpu.make_async_copy(
            wout.at[:, pl.ds(pl.multiple_of(block_of(j) * width, 128), width)],
            wbuf.at[j],
            w_sem.at[j],
        )
        for j in range(blocks)
    ]
    for h in range(min(2, heads)):
        fetch_q(h).start()

    state = hidden[...].astype(F32)
    inv = lax.rsqrt(jnp.mean(state * state, axis=-1, keepdims=True) + 1e-06)
    normed[...] = (state * inv * gain[...]).astype(BF16)

    def rope(u):
        return u * cos[...] + pltpu.roll(u, HD // 2, 1) * sin[...]

    def project(h):
        fetch_q(h).wait()
        qacc[...] = jnp.zeros_like(qacc)

        def step(e, carry):
            prod = jnp.dot(normed[...], wqbuf[h % 2, e], preferred_element_type=F32)
            for s in range(topk):
                qacc[s] = jnp.where(att[:, s : s + 1] == e, prod, qacc[s])
            return carry

        lax.fori_loop(0, experts, step, 0)
        if h + 2 < heads:
            fetch_q(h + 2).start()
        for s in range(topk):
            qall[h][0, s * suffix : (s + 1) * suffix, :] = rope(qacc[s]).astype(BF16)

    def project_keys():
        fetch_k.wait()
        keys = jnp.dot(normed[...], kvbuf[0], preferred_element_type=F32)
        for h in range(heads):
            k_in[h] = rope(keys[:, h * HD : (h + 1) * HD]).astype(BF16)

    def project_values():
        fetch_v.wait()
        vals = jnp.dot(normed[...], kvbuf[1], preferred_element_type=F32)
        for h in range(heads):
            vt_in[h] = vals[:, h * HD : (h + 1) * HD].T.astype(BF16)

    def route():
        logits = jnp.dot(normed[...], router[...], preferred_element_type=F32)
        lane = lax.broadcasted_iota(jnp.int32, logits.shape, 1)
        picks = [
            jnp.sum(jnp.where(lane == att[:, s : s + 1], logits, 0.0), axis=1, keepdims=True)
            for s in range(topk)
        ]
        top = functools.reduce(jnp.maximum, picks)
        raised = [jnp.exp(x - top) for x in picks]
        total = functools.reduce(jnp.add, raised)
        for s in range(topk):
            gates[s * suffix : (s + 1) * suffix, :] = raised[s] / total

    pl.semaphore_wait(barrier, len(partners) + len(mates))

    def gather_copy(h, k):
        n = 2**k
        return pltpu.make_async_remote_copy(
            src_ref=qall[h].at[pl.ds(0, n)],
            dst_ref=qall[h].at[pl.ds(n, n)],
            send_sem=ag_s.at[h, k],
            recv_sem=ag_r.at[h, k],
            device_id=partners[k],
            device_id_type=MESH,
        )

    ust[0] = jnp.zeros_like(ust[0])
    ustat[0, 0:1] = jnp.full((1, qrows), NEG, F32)
    ustat[0, 1:2] = jnp.zeros((1, qrows), F32)

    def scores_t(keys, queries):
        return (
            lax.dot_general(
                keys, queries, (((1,), (1,)), ((), ())), preferred_element_type=F32
            )
            * scale
        )

    def attend(h):
        def unit(u, carry):
            req, page, same = meta[0, u], meta[1, u], meta[2, u]
            s = scores_t(kpool[page, :, h * HD : (h + 1) * HD], qall[h][req])
            m_old = jnp.where(same == 1, ustat[u, 0:1], NEG)
            m_new = jnp.maximum(m_old, jnp.max(s, axis=0, keepdims=True))
            alpha = jnp.exp(m_old - m_new)
            w = jnp.exp(s - m_new)
            ustat[u + 1, 0:1] = m_new
            ustat[u + 1, 1:2] = ustat[u, 1:2] * alpha + jnp.sum(w, axis=0, keepdims=True)
            ust[u + 1] = ust[u] * alpha + jnp.dot(
                vt[h, page], w.astype(BF16), preferred_element_type=F32
            )
            return carry

        lax.fori_loop(0, units, unit, 0, unroll=4)

        def keep(i, carry):
            cur[h, i] = ust[meta[3, i]]
            cstat[h, i] = ustat[meta[3, i]]
            return carry

        lax.fori_loop(0, half, keep, 0)

        def give(i, carry):
            sbuf[h][0][i] = ust[meta[3, half + i]].astype(BF16)
            sstat[h][0][i] = ustat[meta[3, half + i]]
            return carry

        lax.fori_loop(0, half, give, 0)

    def reduce_copies(h, k):
        bit = rounds - 1 - k
        return (
            pltpu.make_async_remote_copy(
                src_ref=sbuf[h][k], dst_ref=rbuf[h][k],
                send_sem=rs_s.at[h, k], recv_sem=rs_r.at[h, k],
                device_id=partners[bit], device_id_type=MESH,
            ),
            pltpu.make_async_remote_copy(
                src_ref=sstat[h][k], dst_ref=rstat[h][k],
                send_sem=rt_s.at[h, k], recv_sem=rt_r.at[h, k],
                device_id=partners[bit], device_id_type=MESH,
            ),
        )

    def merged(m_a, l_a, o_a, m_b, l_b, o_b):
        m = jnp.maximum(m_a, m_b)
        a, b = jnp.exp(m_a - m), jnp.exp(m_b - m)
        return m, l_a * a + l_b * b, o_a * a + o_b * b

    def merge_at(h, k, i):
        return merged(
            cstat[h, i, 0:1], cstat[h, i, 1:2], cur[h, i],
            rstat[h][k][i, 0:1], rstat[h][k][i, 1:2], rbuf[h][k][i].astype(F32),
        )

    slot = lax.broadcasted_iota(jnp.int32, (suffix, qrows), 1) % suffix
    key_at = lax.broadcasted_iota(jnp.int32, (suffix, qrows), 0)
    mask = (key_at <= slot) & (key_at < length[0])

    def pass_on(h, k):
        n = 2 ** (rounds - 2 - k)
        for c in reduce_copies(h, k):
            c.wait_recv()

        def give(i, carry, h=h, k=k, n=n):
            m, l, o = merge_at(h, k, n + i)
            sstat[h][k + 1][i, 0:1] = m
            sstat[h][k + 1][i, 1:2] = l
            sbuf[h][k + 1][i] = o.astype(BF16)
            return carry

        lax.fori_loop(0, n, give, 0)
        for c in reduce_copies(h, k + 1):
            c.start()

        def keep(i, carry, h=h, k=k):
            m, l, o = merge_at(h, k, i)
            cstat[h, i, 0:1] = m
            cstat[h, i, 1:2] = l
            cur[h, i] = o
            return carry

        lax.fori_loop(0, n, keep, 0)
        if k == 0:
            s = jnp.where(mask, scores_t(k_in[h], qall[h][0]), NEG)
            m_s = jnp.max(s, axis=0, keepdims=True)
            w = jnp.exp(s - m_s)
            l_s = jnp.sum(w, axis=0, keepdims=True)
            o_s_ = jnp.dot(vt_in[h], w.astype(BF16), preferred_element_type=F32)
            m, l, o = merged(
                cstat[h, 0, 0:1], cstat[h, 0, 1:2], cur[h, 0], m_s, l_s, o_s_
            )
            cstat[h, 0, 0:1] = m
            cstat[h, 0, 1:2] = l
            cur[h, 0] = o


    for t in range(heads + 2 * rounds - 1):
        for k in range(rounds, -1, -1):
            h = t - k
            if 0 <= h < heads:
                if k > 0:
                    gather_copy(h, k - 1).wait_recv()
                if k < rounds:
                    if k == 0:
                        project(h)
                    gather_copy(h, k).start()
        if t == 0:
            fetch_k.start()
            fetch_v.start()
        if t == 1:
            project_keys()
        if t == 2:
            project_values()
            route()
        if t == max(heads - 1, 2):
            for c in loads:
                c.start()
        if t < heads:
            for p in range(pages):
                vt[t, p] = vpool[p, :, t * HD : (t + 1) * HD].T
        if 0 <= t - rounds < heads:
            attend(t - rounds)
            for c in reduce_copies(t - rounds, 0):
                c.start()
        for k in range(rounds - 2, -1, -1):
            h = t - rounds - 1 - k
            if 0 <= h < heads:
                pass_on(h, k)

    row = lax.broadcasted_iota(jnp.int32, (qrows, 1), 0) % suffix
    factor = gates[...] * (row < length[0]).astype(F32)
    for h in range(heads):
        for c in reduce_copies(h, rounds - 1):
            c.wait_recv()
        m, l, o = merge_at(h, rounds - 1, 0)
        weighted = ((o / l).T * factor).astype(F32)
        for e in range(experts):
            value = jnp.zeros((suffix, HD), F32)
            for s in range(topk):
                value = jnp.where(
                    att[:, s : s + 1] == e, weighted[s * suffix : (s + 1) * suffix], value
                )
            picked[:, (e * heads + h) * HD : (e * heads + h + 1) * HD] = value.astype(BF16)

    depth = heads * HD

    def multiply(j):
        loads[j].wait()
        oacc[...] = jnp.zeros_like(oacc)

        def part(e, carry):
            at = pl.ds(pl.multiple_of(e * depth, depth), depth)
            oacc[...] += jnp.dot(picked[:, at], wbuf[j, at, :], preferred_element_type=F32)
            return carry

        lax.fori_loop(0, experts, part, 0)
        return oacc[...]

    def out_copy(k):
        return pltpu.make_async_remote_copy(
            src_ref=osend[k], dst_ref=orecv[k],
            send_sem=o_s.at[k], recv_sem=o_r.at[k],
            device_id=mates[len(head_bits) - 1 - k], device_id_type=MESH,
        )

    levels = len(head_bits)
    for j in range(blocks // 2, blocks):
        osend[0][j - blocks // 2] = multiply(j).astype(BF16)
    out_copy(0).start()
    for k in range(1, levels):
        n = 2 ** (levels - 1 - k)
        own = [multiply(j) for j in range(n, 2 * n)]
        out_copy(k - 1).wait_recv()
        for j in range(n):
            total = own[j]
            for i in range(k):
                total = total + orecv[i][n + j].astype(F32)
            osend[k][j] = total.astype(BF16)
        out_copy(k).start()
    total = multiply(0)
    out_copy(levels - 1).wait_recv()
    for i in range(levels):
        total = total + orecv[i][0].astype(F32)
    out[...] = total.astype(BF16)

    for k in range(levels):
        out_copy(k).wait_send()
    for h in range(heads):
        for k in range(rounds):
            gather_copy(h, k).wait_send()
            for c in reduce_copies(h, k):
                c.wait_send()


def unit_table(page_table, request_group, deltas, local_pages):
    groups, per_group = page_table.shape
    requests = request_group.shape[0]
    units = local_pages * (requests // groups)
    tok = lax.axis_index("tok")
    order = jnp.bitwise_xor(tok, jnp.asarray(deltas, jnp.int32))
    number = jnp.arange(requests, dtype=jnp.int32)
    group_of = jnp.sum(
        jnp.where(order[:, None] == number[None, :], request_group[None, :], 0), axis=1
    )
    mine = tok * local_pages + jnp.arange(local_pages, dtype=jnp.int32)
    flat = page_table.reshape(-1)
    owner = jnp.arange(flat.shape[0], dtype=jnp.int32) // per_group
    page_group = jnp.sum(jnp.where(flat[None, :] == mine[:, None], owner[None, :], 0), axis=1)
    uses = (group_of[:, None] == page_group[None, :]).astype(jnp.int32).reshape(-1)
    count = uses.shape[0]
    place = jnp.arange(count, dtype=jnp.int32)
    running = jnp.sum(jnp.where(place[None, :] <= place[:, None], uses[None, :], 0), axis=1)
    at = jnp.sum(
        (running[None, :] <= jnp.arange(units, dtype=jnp.int32)[:, None]).astype(jnp.int32), axis=1
    )
    req, page = at // local_pages, at % local_pages
    before = jnp.concatenate([jnp.full((1,), -1, jnp.int32), req[:-1]])
    per = uses.reshape(requests, local_pages)
    ends = running.reshape(requests, local_pages)[:, -1]
    last = jnp.where(jnp.sum(per, axis=1) > 0, ends, 0)
    size = max(units, requests)
    pad = lambda x: jnp.pad(x, (0, size - x.shape[0]))
    return jnp.stack([pad(req), pad(page), pad((req == before).astype(jnp.int32)), pad(last)])


def per_device(
    toks, heads_dev,
    hidden, norm_gain, w_router, w_query, w_key, w_value, w_out,
    key_pool, value_pool, page_table, request_group, suffix_len, att_experts,
):
    rows, model = hidden.shape
    cols = w_key.shape[1]
    heads = cols // HD
    topk = att_experts.shape[1]
    experts = w_query.shape[0]
    prefix = page_table.shape[1] * key_pool.shape[1]
    pages = key_pool.shape[0]
    requests = request_group.shape[0]
    page_rows = key_pool.shape[1]
    qrows = topk * rows
    x = max(toks // 4, 1)
    bits = [1 << n for n in range(toks.bit_length() - 1)]
    tok_bits = [b for b in bits if b >= x] + [b for b in bits if b < x]
    rounds = len(tok_bits)
    deltas = [
        sum(b for n, b in enumerate(tok_bits) if (i >> n) & 1) for i in range(toks)
    ]
    head_bits = [1 << n for n in range(1, heads_dev.bit_length() - 1)] + [1]
    levels = len(head_bits)
    units = pages * (requests // page_table.shape[0])
    meta = unit_table(page_table, request_group, deltas, pages)
    cos, sin = rope_tables(rows, prefix)
    vm = pl.BlockSpec(memory_space=pltpu.VMEM)
    sm = pl.BlockSpec(memory_space=pltpu.SMEM)
    hbm = pl.BlockSpec(memory_space=pl.ANY)
    sizes = [2 ** (rounds - 1 - k_) for k_ in range(rounds)]
    width = model // heads_dev
    dma = pltpu.SemaphoreType.DMA
    scratch = (
        [pltpu.VMEM((toks, qrows, HD), BF16) for _ in range(heads)]
        + [pltpu.VMEM((n, HD, qrows), BF16) for _ in range(heads) for n in sizes]
        + [pltpu.VMEM((n, 2, qrows), F32) for _ in range(heads) for n in sizes]
        + [pltpu.VMEM((n, HD, qrows), BF16) for _ in range(heads) for n in sizes]
        + [pltpu.VMEM((n, 2, qrows), F32) for _ in range(heads) for n in sizes]
        + [
            pltpu.VMEM((heads, pages, HD, page_rows), BF16),
            pltpu.VMEM((units + 1, HD, qrows), F32),
            pltpu.VMEM((units + 1, 2, qrows), F32),
            pltpu.VMEM((heads, sizes[0], HD, qrows), F32),
            pltpu.VMEM((heads, sizes[0], 2, qrows), F32),
            pltpu.VMEM((heads_dev, experts * cols, width), BF16),
            pltpu.VMEM((rows, experts * cols), BF16),
        ]
        + [pltpu.VMEM((2 ** (levels - 1 - k_), rows, width), BF16) for k_ in range(levels)] * 2
        + [
            pltpu.VMEM((rows, width), F32),
            dma((heads, rounds)), dma((heads, rounds)),
            dma((heads, rounds)), dma((heads, rounds)),
            dma((heads, rounds)), dma((heads, rounds)),
            dma((levels,)), dma((levels,)),
            dma((heads_dev,)), dma((2,)), dma((2,)),
            pltpu.VMEM((2, experts, model, HD), BF16),
            pltpu.VMEM((2, model, cols), BF16),
            pltpu.VMEM((rows, model), BF16),
            pltpu.VMEM((topk, rows, HD), F32),
            pltpu.VMEM((heads, rows, HD), BF16),
            pltpu.VMEM((heads, HD, rows), BF16),
            pltpu.VMEM((qrows, 1), F32),
        ]
    )
    return pl.pallas_call(
        functools.partial(attend_kernel, tok_bits, head_bits, units),
        out_shape=jax.ShapeDtypeStruct((rows, width), BF16),
        in_specs=[sm, sm] + [vm] * 8 + [hbm] * 4,
        out_specs=vm,
        scratch_shapes=scratch,
        compiler_params=pltpu.CompilerParams(
            collective_id=0, has_side_effects=True, vmem_limit_bytes=56 * 2**20
        ),
        name="layer",
    )(
        meta, suffix_len, hidden, norm_gain.reshape(1, -1), w_router, att_experts,
        jnp.asarray(cos), jnp.asarray(sin), key_pool, value_pool, w_query, w_key, w_value,
        w_out.reshape(experts * cols, model),
    )


def solution(mesh):
    return jax.shard_map(
        functools.partial(per_device, mesh.shape["tok"], mesh.shape["head"]),
        mesh=mesh,
        in_specs=(
            P("tok", None), P(), P(), P(None, None, "head"), P(None, "head"), P(None, "head"),
            P(None, "head", None), P("tok", None, "head"), P("tok", None, "head"),
            P(), P(), P("tok"), P("tok", None),
        ),
        out_specs=P("tok", "head"),
        check_vma=False,
    )
```

```python
import functools

import jax
import jax.numpy as jnp
import numpy as np
from jax import lax
from jax.experimental import pallas as pl
from jax.experimental.pallas import tpu as pltpu
from jax.sharding import PartitionSpec as P

HD = 128
F32 = jnp.float32
BF16 = jnp.bfloat16
NEG = -1e30
MESH = pl.DeviceIdType.MESH


def rope_tables(rows, first):
    half = HD // 2
    freq = (10000.0 ** (-np.arange(half, dtype=np.float64) * 2.0 / HD)).astype(np.float32)
    angle = (np.arange(rows, dtype=np.float32)[:, None] + np.float32(first)) * freq[None, :]
    cosine, sine = np.cos(angle), np.sin(angle)
    return (
        np.concatenate([cosine, cosine], axis=1).astype(np.float32),
        np.concatenate([-sine, sine], axis=1).astype(np.float32),
    )


def attend_kernel(
    tok_bits, head_bits, units,
    meta, length, hidden, gain, router, att, cos, sin, kpool, vpool, wq, wk, wv, wout,
    out,
    *scratch,
):
    suffix = hidden.shape[0]
    topk = att.shape[1]
    qrows = topk * suffix
    heads = wk.shape[1] // HD
    pages = kpool.shape[0]
    rounds = len(tok_bits)
    half = 2 ** (rounds - 1)
    experts = wout.shape[0] // (heads * HD)
    scale = 1.0 / HD**0.5
    blocks = 2 ** len(head_bits)
    width = wout.shape[1] // blocks

    it = iter(scratch)
    qall = [next(it) for _ in range(heads)]
    sbuf = [[next(it) for _ in range(rounds)] for _ in range(heads)]
    sstat = [[next(it) for _ in range(rounds)] for _ in range(heads)]
    rbuf = [[next(it) for _ in range(rounds)] for _ in range(heads)]
    rstat = [[next(it) for _ in range(rounds)] for _ in range(heads)]
    vt = next(it)
    ust = next(it)
    ustat = next(it)
    cur = next(it)
    cstat = next(it)
    wbuf = next(it)
    picked = next(it)
    osend = [next(it) for _ in head_bits]
    orecv = [next(it) for _ in head_bits]
    oacc = next(it)
    ag_s, ag_r = next(it), next(it)
    rs_s, rs_r = next(it), next(it)
    rt_s, rt_r = next(it), next(it)
    o_s, o_r = next(it), next(it)
    w_sem = next(it)
    q_sem = next(it)
    kv_sem = next(it)
    wqbuf, kvbuf, normed, qacc, k_in, vt_in, gates = [next(it) for _ in range(7)]

    tok = lax.axis_index("tok")
    head = lax.axis_index("head")

    def flip(index, bit):
        return index + bit * (1 - 2 * ((index // bit) % 2))

    partners = [{"tok": flip(tok, b)} for b in tok_bits]
    mates = [{"head": flip(head, b)} for b in head_bits]

    barrier = pltpu.get_barrier_semaphore()
    for other in partners + mates:
        pl.semaphore_signal(barrier, inc=1, device_id=other, device_id_type=MESH)

    def block_of(j):
        col = head
        for n, b in enumerate(head_bits):
            if (j >> n) & 1:
                col = flip(col, b)
        return col

    def fetch_q(h):
        return pltpu.make_async_copy(
            wq.at[:, :, pl.ds(h * HD, HD)], wqbuf.at[h % 2], q_sem.at[h % 2]
        )

    fetch_k = pltpu.make_async_copy(wk, kvbuf.at[0], kv_sem.at[0])
    fetch_v = pltpu.make_async_copy(wv, kvbuf.at[1], kv_sem.at[1])
    loads = [
        pltpu.make_async_copy(
            wout.at[:, pl.ds(pl.multiple_of(block_of(j) * width, 128), width)],
            wbuf.at[j],
            w_sem.at[j],
        )
        for j in range(blocks)
    ]
    for h in range(min(2, heads)):
        fetch_q(h).start()

    state = hidden[...].astype(F32)
    inv = lax.rsqrt(jnp.mean(state * state, axis=-1, keepdims=True) + 1e-06)
    normed[...] = (state * inv * gain[...]).astype(BF16)

    def rope(u):
        return u * cos[...] + pltpu.roll(u, HD // 2, 1) * sin[...]

    def project(h):
        fetch_q(h).wait()
        qacc[...] = jnp.zeros_like(qacc)

        def step(e, carry):
            prod = jnp.dot(normed[...], wqbuf[h % 2, e], preferred_element_type=F32)
            for s in range(topk):
                qacc[s] = jnp.where(att[:, s : s + 1] == e, prod, qacc[s])
            return carry

        lax.fori_loop(0, experts, step, 0)
        if h + 2 < heads:
            fetch_q(h + 2).start()
        for s in range(topk):
            qall[h][0, s * suffix : (s + 1) * suffix, :] = rope(qacc[s]).astype(BF16)

    def project_keys():
        fetch_k.wait()
        keys = jnp.dot(normed[...], kvbuf[0], preferred_element_type=F32)
        for h in range(heads):
            k_in[h] = rope(keys[:, h * HD : (h + 1) * HD]).astype(BF16)

    def project_values():
        fetch_v.wait()
        vals = jnp.dot(normed[...], kvbuf[1], preferred_element_type=F32)
        for h in range(heads):
            vt_in[h] = vals[:, h * HD : (h + 1) * HD].T.astype(BF16)

    def route():
        logits = jnp.dot(normed[...], router[...], preferred_element_type=F32)
        lane = lax.broadcasted_iota(jnp.int32, logits.shape, 1)
        picks = [
            jnp.sum(jnp.where(lane == att[:, s : s + 1], logits, 0.0), axis=1, keepdims=True)
            for s in range(topk)
        ]
        top = functools.reduce(jnp.maximum, picks)
        raised = [jnp.exp(x - top) for x in picks]
        total = functools.reduce(jnp.add, raised)
        for s in range(topk):
            gates[s * suffix : (s + 1) * suffix, :] = raised[s] / total

    pl.semaphore_wait(barrier, len(partners) + len(mates))

    def gather_copy(h, k):
        n = 2**k
        return pltpu.make_async_remote_copy(
            src_ref=qall[h].at[pl.ds(0, n)],
            dst_ref=qall[h].at[pl.ds(n, n)],
            send_sem=ag_s.at[h, k],
            recv_sem=ag_r.at[h, k],
            device_id=partners[k],
            device_id_type=MESH,
        )

    ust[0] = jnp.zeros_like(ust[0])
    ustat[0, 0:1] = jnp.full((1, qrows), NEG, F32)
    ustat[0, 1:2] = jnp.zeros((1, qrows), F32)

    def scores_t(keys, queries):
        return (
            lax.dot_general(
                keys, queries, (((1,), (1,)), ((), ())), preferred_element_type=F32
            )
            * scale
        )

    def attend(h):
        def unit(u, carry):
            req, page, same = meta[0, u], meta[1, u], meta[2, u]
            s = scores_t(kpool[page, :, h * HD : (h + 1) * HD], qall[h][req])
            m_old = jnp.where(same == 1, ustat[u, 0:1], NEG)
            m_new = jnp.maximum(m_old, jnp.max(s, axis=0, keepdims=True))
            alpha = jnp.exp(m_old - m_new)
            w = jnp.exp(s - m_new)
            ustat[u + 1, 0:1] = m_new
            ustat[u + 1, 1:2] = ustat[u, 1:2] * alpha + jnp.sum(w, axis=0, keepdims=True)
            ust[u + 1] = ust[u] * alpha + jnp.dot(
                vt[h, page], w.astype(BF16), preferred_element_type=F32
            )
            return carry

        lax.fori_loop(0, units, unit, 0, unroll=True)

        def keep(i, carry):
            cur[h, i] = ust[meta[3, i]]
            cstat[h, i] = ustat[meta[3, i]]
            return carry

        lax.fori_loop(0, half, keep, 0)

        def give(i, carry):
            sbuf[h][0][i] = ust[meta[3, half + i]].astype(BF16)
            sstat[h][0][i] = ustat[meta[3, half + i]]
            return carry

        lax.fori_loop(0, half, give, 0)

    def reduce_copies(h, k):
        bit = rounds - 1 - k
        return (
            pltpu.make_async_remote_copy(
                src_ref=sbuf[h][k], dst_ref=rbuf[h][k],
                send_sem=rs_s.at[h, k], recv_sem=rs_r.at[h, k],
                device_id=partners[bit], device_id_type=MESH,
            ),
            pltpu.make_async_remote_copy(
                src_ref=sstat[h][k], dst_ref=rstat[h][k],
                send_sem=rt_s.at[h, k], recv_sem=rt_r.at[h, k],
                device_id=partners[bit], device_id_type=MESH,
            ),
        )

    def merged(m_a, l_a, o_a, m_b, l_b, o_b):
        m = jnp.maximum(m_a, m_b)
        a, b = jnp.exp(m_a - m), jnp.exp(m_b - m)
        return m, l_a * a + l_b * b, o_a * a + o_b * b

    def merge_at(h, k, i):
        return merged(
            cstat[h, i, 0:1], cstat[h, i, 1:2], cur[h, i],
            rstat[h][k][i, 0:1], rstat[h][k][i, 1:2], rbuf[h][k][i].astype(F32),
        )

    slot = lax.broadcasted_iota(jnp.int32, (suffix, qrows), 1) % suffix
    key_at = lax.broadcasted_iota(jnp.int32, (suffix, qrows), 0)
    mask = (key_at <= slot) & (key_at < length[0])

    def pass_on(h, k):
        n = 2 ** (rounds - 2 - k)
        for c in reduce_copies(h, k):
            c.wait_recv()

        def give(i, carry, h=h, k=k, n=n):
            m, l, o = merge_at(h, k, n + i)
            sstat[h][k + 1][i, 0:1] = m
            sstat[h][k + 1][i, 1:2] = l
            sbuf[h][k + 1][i] = o.astype(BF16)
            return carry

        lax.fori_loop(0, n, give, 0)
        for c in reduce_copies(h, k + 1):
            c.start()

        def keep(i, carry, h=h, k=k):
            m, l, o = merge_at(h, k, i)
            cstat[h, i, 0:1] = m
            cstat[h, i, 1:2] = l
            cur[h, i] = o
            return carry

        lax.fori_loop(0, n, keep, 0)
        if k == 0:
            s = jnp.where(mask, scores_t(k_in[h], qall[h][0]), NEG)
            m_s = jnp.max(s, axis=0, keepdims=True)
            w = jnp.exp(s - m_s)
            l_s = jnp.sum(w, axis=0, keepdims=True)
            o_s_ = jnp.dot(vt_in[h], w.astype(BF16), preferred_element_type=F32)
            m, l, o = merged(
                cstat[h, 0, 0:1], cstat[h, 0, 1:2], cur[h, 0], m_s, l_s, o_s_
            )
            cstat[h, 0, 0:1] = m
            cstat[h, 0, 1:2] = l
            cur[h, 0] = o


    for t in range(heads + 2 * rounds - 1):
        for k in range(rounds, -1, -1):
            h = t - k
            if 0 <= h < heads:
                if k > 0:
                    gather_copy(h, k - 1).wait_recv()
                if k < rounds:
                    if k == 0:
                        project(h)
                    gather_copy(h, k).start()
        if t == 0:
            fetch_k.start()
            fetch_v.start()
        if t == 1:
            project_keys()
        if t == 2:
            project_values()
            route()
        if t == max(heads - 1, 2):
            for c in loads:
                c.start()
        if t < heads:
            for p in range(pages):
                vt[t, p] = vpool[p, :, t * HD : (t + 1) * HD].T
        if 0 <= t - rounds < heads:
            attend(t - rounds)
            for c in reduce_copies(t - rounds, 0):
                c.start()
        for k in range(rounds - 2, -1, -1):
            h = t - rounds - 1 - k
            if 0 <= h < heads:
                pass_on(h, k)

    row = lax.broadcasted_iota(jnp.int32, (qrows, 1), 0) % suffix
    factor = gates[...] * (row < length[0]).astype(F32)
    for h in range(heads):
        for c in reduce_copies(h, rounds - 1):
            c.wait_recv()
        m, l, o = merge_at(h, rounds - 1, 0)
        weighted = ((o / l).T * factor).astype(F32)
        for e in range(experts):
            value = jnp.zeros((suffix, HD), F32)
            for s in range(topk):
                value = jnp.where(
                    att[:, s : s + 1] == e, weighted[s * suffix : (s + 1) * suffix], value
                )
            picked[:, (e * heads + h) * HD : (e * heads + h + 1) * HD] = value.astype(BF16)

    depth = heads * HD

    def multiply(j):
        loads[j].wait()
        oacc[...] = jnp.zeros_like(oacc)

        def part(e, carry):
            at = pl.ds(pl.multiple_of(e * depth, depth), depth)
            oacc[...] += jnp.dot(picked[:, at], wbuf[j, at, :], preferred_element_type=F32)
            return carry

        lax.fori_loop(0, experts, part, 0)
        return oacc[...]

    def out_copy(k):
        return pltpu.make_async_remote_copy(
            src_ref=osend[k], dst_ref=orecv[k],
            send_sem=o_s.at[k], recv_sem=o_r.at[k],
            device_id=mates[len(head_bits) - 1 - k], device_id_type=MESH,
        )

    levels = len(head_bits)
    for j in range(blocks // 2, blocks):
        osend[0][j - blocks // 2] = multiply(j).astype(BF16)
    out_copy(0).start()
    for k in range(1, levels):
        n = 2 ** (levels - 1 - k)
        own = [multiply(j) for j in range(n, 2 * n)]
        out_copy(k - 1).wait_recv()
        for j in range(n):
            total = own[j]
            for i in range(k):
                total = total + orecv[i][n + j].astype(F32)
            osend[k][j] = total.astype(BF16)
        out_copy(k).start()
    total = multiply(0)
    out_copy(levels - 1).wait_recv()
    for i in range(levels):
        total = total + orecv[i][0].astype(F32)
    out[...] = total.astype(BF16)

    for k in range(levels):
        out_copy(k).wait_send()
    for h in range(heads):
        for k in range(rounds):
            gather_copy(h, k).wait_send()
            for c in reduce_copies(h, k):
                c.wait_send()


def unit_table(page_table, request_group, deltas, local_pages):
    groups, per_group = page_table.shape
    requests = request_group.shape[0]
    units = local_pages * (requests // groups)
    tok = lax.axis_index("tok")
    order = jnp.bitwise_xor(tok, jnp.asarray(deltas, jnp.int32))
    number = jnp.arange(requests, dtype=jnp.int32)
    group_of = jnp.sum(
        jnp.where(order[:, None] == number[None, :], request_group[None, :], 0), axis=1
    )
    mine = tok * local_pages + jnp.arange(local_pages, dtype=jnp.int32)
    flat = page_table.reshape(-1)
    owner = jnp.arange(flat.shape[0], dtype=jnp.int32) // per_group
    page_group = jnp.sum(jnp.where(flat[None, :] == mine[:, None], owner[None, :], 0), axis=1)
    uses = (group_of[:, None] == page_group[None, :]).astype(jnp.int32).reshape(-1)
    count = uses.shape[0]
    place = jnp.arange(count, dtype=jnp.int32)
    running = jnp.sum(jnp.where(place[None, :] <= place[:, None], uses[None, :], 0), axis=1)
    at = jnp.sum(
        (running[None, :] <= jnp.arange(units, dtype=jnp.int32)[:, None]).astype(jnp.int32), axis=1
    )
    req, page = at // local_pages, at % local_pages
    before = jnp.concatenate([jnp.full((1,), -1, jnp.int32), req[:-1]])
    per = uses.reshape(requests, local_pages)
    ends = running.reshape(requests, local_pages)[:, -1]
    last = jnp.where(jnp.sum(per, axis=1) > 0, ends, 0)
    size = max(units, requests)
    pad = lambda x: jnp.pad(x, (0, size - x.shape[0]))
    return jnp.stack([pad(req), pad(page), pad((req == before).astype(jnp.int32)), pad(last)])


def per_device(
    toks, heads_dev,
    hidden, norm_gain, w_router, w_query, w_key, w_value, w_out,
    key_pool, value_pool, page_table, request_group, suffix_len, att_experts,
):
    rows, model = hidden.shape
    cols = w_key.shape[1]
    heads = cols // HD
    topk = att_experts.shape[1]
    experts = w_query.shape[0]
    prefix = page_table.shape[1] * key_pool.shape[1]
    pages = key_pool.shape[0]
    requests = request_group.shape[0]
    page_rows = key_pool.shape[1]
    qrows = topk * rows
    x = max(toks // 4, 1)
    bits = [1 << n for n in range(toks.bit_length() - 1)]
    tok_bits = [b for b in bits if b >= x] + [b for b in bits if b < x]
    rounds = len(tok_bits)
    deltas = [
        sum(b for n, b in enumerate(tok_bits) if (i >> n) & 1) for i in range(toks)
    ]
    head_bits = [1 << n for n in range(1, heads_dev.bit_length() - 1)] + [1]
    levels = len(head_bits)
    units = pages * (requests // page_table.shape[0])
    meta = unit_table(page_table, request_group, deltas, pages)
    cos, sin = rope_tables(rows, prefix)
    vm = pl.BlockSpec(memory_space=pltpu.VMEM)
    sm = pl.BlockSpec(memory_space=pltpu.SMEM)
    hbm = pl.BlockSpec(memory_space=pl.ANY)
    sizes = [2 ** (rounds - 1 - k_) for k_ in range(rounds)]
    width = model // heads_dev
    dma = pltpu.SemaphoreType.DMA
    scratch = (
        [pltpu.VMEM((toks, qrows, HD), BF16) for _ in range(heads)]
        + [pltpu.VMEM((n, HD, qrows), BF16) for _ in range(heads) for n in sizes]
        + [pltpu.VMEM((n, 2, qrows), F32) for _ in range(heads) for n in sizes]
        + [pltpu.VMEM((n, HD, qrows), BF16) for _ in range(heads) for n in sizes]
        + [pltpu.VMEM((n, 2, qrows), F32) for _ in range(heads) for n in sizes]
        + [
            pltpu.VMEM((heads, pages, HD, page_rows), BF16),
            pltpu.VMEM((units + 1, HD, qrows), F32),
            pltpu.VMEM((units + 1, 2, qrows), F32),
            pltpu.VMEM((heads, sizes[0], HD, qrows), F32),
            pltpu.VMEM((heads, sizes[0], 2, qrows), F32),
            pltpu.VMEM((heads_dev, experts * cols, width), BF16),
            pltpu.VMEM((rows, experts * cols), BF16),
        ]
        + [pltpu.VMEM((2 ** (levels - 1 - k_), rows, width), BF16) for k_ in range(levels)] * 2
        + [
            pltpu.VMEM((rows, width), F32),
            dma((heads, rounds)), dma((heads, rounds)),
            dma((heads, rounds)), dma((heads, rounds)),
            dma((heads, rounds)), dma((heads, rounds)),
            dma((levels,)), dma((levels,)),
            dma((heads_dev,)), dma((2,)), dma((2,)),
            pltpu.VMEM((2, experts, model, HD), BF16),
            pltpu.VMEM((2, model, cols), BF16),
            pltpu.VMEM((rows, model), BF16),
            pltpu.VMEM((topk, rows, HD), F32),
            pltpu.VMEM((heads, rows, HD), BF16),
            pltpu.VMEM((heads, HD, rows), BF16),
            pltpu.VMEM((qrows, 1), F32),
        ]
    )
    return pl.pallas_call(
        functools.partial(attend_kernel, tok_bits, head_bits, units),
        out_shape=jax.ShapeDtypeStruct((rows, width), BF16),
        in_specs=[sm, sm] + [vm] * 8 + [hbm] * 4,
        out_specs=vm,
        scratch_shapes=scratch,
        compiler_params=pltpu.CompilerParams(
            collective_id=0, has_side_effects=True, vmem_limit_bytes=56 * 2**20
        ),
        name="layer",
    )(
        meta, suffix_len, hidden, norm_gain.reshape(1, -1), w_router, att_experts,
        jnp.asarray(cos), jnp.asarray(sin), key_pool, value_pool, w_query, w_key, w_value,
        w_out.reshape(experts * cols, model),
    )


def solution(mesh):
    return jax.shard_map(
        functools.partial(per_device, mesh.shape["tok"], mesh.shape["head"]),
        mesh=mesh,
        in_specs=(
            P("tok", None), P(), P(), P(None, None, "head"), P(None, "head"), P(None, "head"),
            P(None, "head", None), P("tok", None, "head"), P("tok", None, "head"),
            P(), P(), P("tok"), P("tok", None),
        ),
        out_specs=P("tok", "head"),
        check_vma=False,
    )
```
